32 devices in a mesh: groups: 2 (over x), row: 16 (over z, y, core).
Axes of the slice: x: 2, y: 2, z: 4, core: 2. Of those that a mesh axis runs over, the one named last changes fastest.
Arguments:
- gate_pre: bfloat16 [4096, 14336], P(('groups', 'row')), parts along dimension 0, may hold values from -8 to 8
- up_pre: bfloat16 [4096, 14336], P(('groups', 'row')), parts along dimension 0, may hold values from -6 to 6
- out_grad: bfloat16 [4096, 4096], P(('groups', 'row')), parts along dimension 0, may hold values from -6 to 6
- down_weight: bfloat16 [14336, 4096], P('row'), may hold values from -0.046875 to 0.046875
Outputs:
- weight_grad: bfloat16 [28672, 4096], P(('groups', 'row')), parts along dimension 0
- gate_grad: bfloat16 [4096, 14336], P(('groups', 'row')), parts along dimension 0
- up_grad: bfloat16 [4096, 14336], P(('groups', 'row')), parts along dimension 0
The draws below stay inside these ranges and needn't reach their ends.
There are 2 independent parts, one for each index of `groups`. The reference program is written for one: setup_inputs(seed, part) draws one part's arguments, and reference() takes and returns one part's arrays. A program takes and returns all parts, laid end to end along the dimension named above; an argument that names none is the same for every part. Nothing has to cross between parts.
All inputs are finite; a program needn't handle non-finite values.
Results may differ from the reference program's by a relative error of at most 0.005.
Values may be sent and summed in bfloat16 or wider, within the bound.
A program may use at most 128 MiB of HBM per device.

```python
import jax
import jax.numpy as jnp

D = 4096
FF = 14336
TOKENS = 2048


def shard_levels(stream_key, shape, shards, low, largest):
    def one(axis_at, parts):
        steps = jax.random.uniform(jax.random.fold_in(jax.random.fold_in(stream_key, 6), axis_at), (parts,), jnp.float32, low / len(shards), largest / len(shards))
        return jnp.repeat(jnp.exp(steps), shape[axis_at] // parts).reshape((-1,) + (1,) * (len(shape) - axis_at - 1))

    factor_of = one(*shards[0])
    for cut in shards[1:]:
        factor_of = factor_of * one(*cut)
    return factor_of


def bell_draw(rng, shape, width, bound, pieces=(), dtype=jnp.bfloat16):
    drawn = width * jax.random.normal(rng, shape, jnp.float32)
    if pieces:
        drawn = drawn * shard_levels(rng, shape, pieces, -0.22, 0.18)
    return jnp.clip(drawn, -bound, bound).astype(dtype)


def setup_inputs(seed: int = 0, part: int = 0) -> dict:
    seeds = jax.random.split(jax.random.key(seed), 5)
    part_splits = jax.random.split(jax.random.fold_in(seeds[4], part), 5)
    gate_pre = bell_draw(part_splits[0], (TOKENS, FF), 1.5, 8.0, ((0, 16),))
    up_pre = bell_draw(part_splits[1], (TOKENS, FF), 1.0, 6.0, ((0, 16),))
    out_grad = bell_draw(part_splits[2], (TOKENS, D), 1.0, 6.0, ((0, 16),))
    down_weight = bell_draw(seeds[3], (FF, D), FF ** -0.5, 0.046875, ((0, 16),))
    return dict(gate_pre=gate_pre, up_pre=up_pre, out_grad=out_grad, down_weight=down_weight)


def reference(gate_pre, up_pre, out_grad, down_weight):
    gate_wide = gate_pre.astype(jnp.float32)
    up_wide = up_pre.astype(jnp.float32)
    hidden = (jax.nn.silu(gate_wide) * up_wide).astype(jnp.bfloat16)
    weight_grad = jnp.dot(hidden.T, out_grad, preferred_element_type=jnp.float32).astype(jnp.bfloat16)
    hidden_grad = jnp.dot(out_grad, down_weight.T, preferred_element_type=jnp.float32).astype(jnp.bfloat16)
    grad_wide = hidden_grad.astype(jnp.float32)
    sigmoid = 1.0 / (1.0 + jnp.exp(-gate_wide))
    up_grad = (grad_wide * gate_wide * sigmoid).astype(jnp.bfloat16)
    gate_grad = (grad_wide * up_wide * sigmoid * (1.0 + gate_wide * (1.0 - sigmoid))).astype(jnp.bfloat16)
    return weight_grad, gate_grad, up_grad
```

```python
import functools

import jax
import jax.numpy as jnp
from jax import lax
from jax.experimental import pallas as pl
from jax.experimental.pallas import tpu as pltpu
from jax.sharding import PartitionSpec as P

MESH = pl.DeviceIdType.MESH
TILE = 256


def cols(ref, at, ff):
    if len(ref.shape) == 3:
        return ref.at[at]
    return ref.at[:, pl.ds(pl.multiple_of(at * ff, 128), ff)]


def kernel(
    A, B, hid_ref, og_ref, w_ref, wg_ref, gr_ref, og_all, w_v, hid_v, hid_t, gcols, wg_v,
    local_sem, ag_recv, z_send, y_send, c_send, h_send, h_recv, g_send, g_recv, out_sem,
):
    n = A * B * 2
    ff, depth = w_ref.shape
    rows = og_ref.shape[0]
    me = lax.axis_index("row")
    z, y, c = me // (2 * B), (me // 2) % B, me % 2

    def idx(zz, yy, cc):
        return (zz * B + yy) * 2 + cc

    own_og = pltpu.make_async_copy(og_ref, og_all.at[me], local_sem.at[0])
    own_w = pltpu.make_async_copy(w_ref, w_v, local_sem.at[1])
    own_hid = pltpu.make_async_copy(cols(hid_ref, me, ff), hid_v.at[me], local_sem.at[2])
    own_grad = pltpu.make_async_copy(gcols.at[me], cols(gr_ref, me, ff), local_sem.at[3])
    own_og.start()
    own_w.start()
    own_hid.start()

    barrier = pltpu.get_barrier_semaphore()

    @pl.loop(1, n)
    def _(k):
        pl.semaphore_signal(barrier, inc=1, device_id={"row": (me + k) % n}, device_id_type=MESH)

    pl.semaphore_wait(barrier, n - 1)

    def shard_copy(owner, target, send):
        return pltpu.make_async_remote_copy(
            og_all.at[owner], og_all.at[owner], send, ag_recv.at[owner],
            device_id={"row": target}, device_id_type=MESH,
        )

    def down(zp):
        return shard_copy(idx(zp, y, c), idx((z + A - 1) % A, y, c), z_send.at[zp])

    def up(zp):
        return shard_copy(idx(zp, y, c), idx((z + 1) % A, y, c), z_send.at[A + zp])

    def across(zp):
        return shard_copy(idx(zp, y, c), idx(z, (y + 1) % B, c), y_send.at[zp])

    def beside(zp, yp):
        return shard_copy(idx(zp, yp, c), idx(z, y, 1 - c), c_send.at[zp * B + yp])

    def hidden_copy(k):
        to = (me + k) % n
        return pltpu.make_async_remote_copy(
            cols(hid_ref, to, ff), hid_v.at[me], h_send.at[k], h_recv.at[me],
            device_id={"row": to}, device_id_type=MESH,
        )

    def grad_copy(owner):
        return pltpu.make_async_remote_copy(
            gcols.at[owner], cols(gr_ref, me, ff), g_send.at[owner], g_recv.at[me],
            device_id={"row": owner}, device_id_type=MESH,
        )

    def wait_shard(owner):
        pltpu.make_async_copy(og_all.at[owner], og_all.at[owner], ag_recv.at[owner]).wait()

    def forward(zp, first):
        if not first:
            wait_shard(idx(zp, y, c))

        @pl.when((zp >= z) & (z > 0))
        def _():
            down(zp).start()

        @pl.when((zp <= z) & (z < A - 1))
        def _():
            up(zp).start()

        if B > 1:
            across(zp).start()
        beside(zp, y).start()

    def forward_across(zp):
        if B > 1:
            other = (y + 1) % B
            wait_shard(idx(zp, other, c))
            beside(zp, other).start()

    own_og.wait()
    forward(z, True)
    share = -(-(n - 1) // A)

    @pl.loop(0, A)
    def _(d):
        for sign in (1, -1):
            zp = z + sign * d

            @pl.when((d > 0) & (zp >= 0) & (zp < A))
            def _():
                forward(zp, False)

        @pl.loop(0, share)
        def _(i):
            k = d * share + i + 1

            @pl.when(k < n)
            def _():
                hidden_copy(k).start()

        @pl.when(d == 0)
        def _():
            own_w.wait()
            forward_across(z)

        for sign in (1, -1):
            zp = z + sign * d

            @pl.when((d > 0) & (zp >= 0) & (zp < A))
            def _():
                forward_across(zp)

        @pl.loop(0, 4 * B)
        def _(j):
            sign = 1 - 2 * (j // (2 * B))
            r = j % (2 * B)
            zp = z + sign * d

            @pl.when((zp >= 0) & (zp < A) & ((d > 0) | (j < 2 * B)))
            def _():
                owner = idx(zp, (y + r) % B, (c + r // B) % 2)

                @pl.when(r >= B)
                def _():
                    wait_shard(owner)

                gcols[owner] = lax.dot_general(
                    og_all[owner], w_v[...], (((1,), (1,)), ((), ())),
                    preferred_element_type=jnp.float32,
                ).astype(gcols.dtype)

                @pl.when(owner == me)
                def _():
                    own_grad.start()

                @pl.when(owner != me)
                def _():
                    grad_copy(owner).start()

    own_hid.wait()

    @pl.loop(0, n)
    def _(k):
        src = (me + k) % n

        @pl.when(k > 0)
        def _():
            pltpu.make_async_copy(hid_v.at[src], hid_v.at[src], h_recv.at[src]).wait()

        hid_t[:, pl.ds(pl.multiple_of(src * rows, 128), rows)] = hid_v[src].T

    def out_copy(t):
        at = pl.ds(pl.multiple_of(t * TILE, TILE), TILE)
        return pltpu.make_async_copy(wg_v.at[:, at], wg_ref.at[:, at], out_sem.at[t])

    @pl.loop(0, depth // TILE)
    def _(t):
        at = pl.ds(pl.multiple_of(t * TILE, TILE), TILE)
        wg_v[:, at] = lax.dot_general(
            hid_t[...], og_all[:, :, at].reshape(n * rows, TILE), (((1,), (0,)), ((), ())),
            preferred_element_type=jnp.float32,
        ).astype(wg_v.dtype)
        out_copy(t).start()

    @pl.loop(0, A)
    def _(zp):
        @pl.when((zp >= z) & (z > 0))
        def _():
            down(zp).wait_send()

        @pl.when((zp <= z) & (z < A - 1))
        def _():
            up(zp).wait_send()

        if B > 1:
            across(zp).wait_send()
        for yp in range(B):
            beside(zp, yp).wait_send()

    @pl.loop(0, depth // TILE)
    def _(t):
        out_copy(t).wait()

    @pl.loop(1, n)
    def _(k):
        hidden_copy(k).wait_send()
        grad_copy((me + k) % n).wait_send()

    own_grad.wait()

    @pl.loop(1, n)
    def _(k):
        src = (me + k) % n
        pltpu.make_async_copy(cols(gr_ref, src, ff), cols(gr_ref, src, ff), g_recv.at[src]).wait()


def local(n, gate_pre, up_pre, out_grad, down_weight):
    rows, width = gate_pre.shape
    ff, depth = down_weight.shape
    B = 2 if n == 16 else 1
    A = n // (2 * B)
    flat = ff % 128 == 0
    gate_wide = gate_pre.astype(jnp.float32)
    up_wide = up_pre.astype(jnp.float32)
    hidden = (jax.nn.silu(gate_wide) * up_wide).astype(jnp.bfloat16)
    if not flat:
        hidden = hidden.reshape(rows, n, ff).transpose(1, 0, 2)
    bf16 = jnp.bfloat16
    dma = pltpu.SemaphoreType.DMA
    weight_grad, grad_rows = pl.pallas_call(
        functools.partial(kernel, A, B),
        out_shape=(
            jax.ShapeDtypeStruct((ff, depth), bf16),
            jax.ShapeDtypeStruct((rows, width) if flat else (n, rows, ff), bf16),
        ),
        in_specs=[pl.BlockSpec(memory_space=pl.ANY)] * 3,
        out_specs=(pl.BlockSpec(memory_space=pl.ANY),) * 2,
        scratch_shapes=[
            pltpu.VMEM((n, rows, depth), bf16),
            pltpu.VMEM((ff, depth), bf16),
            pltpu.VMEM((n, rows, ff), bf16),
            pltpu.VMEM((ff, n * rows), bf16),
            pltpu.VMEM((n, rows, ff), bf16),
            pltpu.VMEM((ff, depth), bf16),
            dma((4,)),
            dma((n,)),
            dma((2 * A,)),
            dma((A,)),
            dma((n // 2,)),
            dma((n,)),
            dma((n,)),
            dma((n,)),
            dma((n,)),
            dma((depth // TILE,)),
        ],
        compiler_params=pltpu.CompilerParams(
            collective_id=0, has_side_effects=True, vmem_limit_bytes=60 * 2**20
        ),
        name="swiglu_backward",
    )(hidden, out_grad, down_weight)
    if not flat:
        grad_rows = grad_rows.transpose(1, 0, 2).reshape(rows, width)
    grad_wide = grad_rows.astype(jnp.float32)
    sigmoid = 1.0 / (1.0 + jnp.exp(-gate_wide))
    up_grad = (grad_wide * gate_wide * sigmoid).astype(bf16)
    gate_grad = (grad_wide * up_wide * sigmoid * (1.0 + gate_wide * (1.0 - sigmoid))).astype(bf16)
    return (weight_grad, gate_grad, up_grad)


def solution(mesh):
    return jax.shard_map(
        functools.partial(local, mesh.shape["row"]),
        mesh=mesh,
        in_specs=(
            P(("groups", "row"), None),
            P(("groups", "row"), None),
            P(("groups", "row"), None),
            P("row", None),
        ),
        out_specs=(
            P(("groups", "row"), None),
            P(("groups", "row"), None),
            P(("groups", "row"), None),
        ),
        check_vma=False,
    )
```

```python
import functools

import jax
import jax.numpy as jnp
from jax import lax
from jax.experimental import pallas as pl
from jax.experimental.pallas import tpu as pltpu
from jax.sharding import PartitionSpec as P

MESH = pl.DeviceIdType.MESH
TILE = 256


def cols(ref, at, ff):
    if len(ref.shape) == 3:
        return ref.at[at]
    return ref.at[:, pl.ds(pl.multiple_of(at * ff, 128), ff)]


def kernel(
    A, B, hid_ref, og_ref, w_ref, wg_ref, gr_ref, og_all, w_v, hid_v, hid_t, gcols, wg_v,
    local_sem, ag_recv, z_send, y_send, c_send, h_send, h_recv, g_send, g_recv, out_sem,
):
    n = A * B * 2
    ff, depth = w_ref.shape
    rows = og_ref.shape[0]
    me = lax.axis_index("row")
    z, y, c = me // (2 * B), (me // 2) % B, me % 2

    def idx(zz, yy, cc):
        return (zz * B + yy) * 2 + cc

    own_og = pltpu.make_async_copy(og_ref, og_all.at[me], local_sem.at[0])
    own_w = pltpu.make_async_copy(w_ref, w_v, local_sem.at[1])
    own_hid = pltpu.make_async_copy(cols(hid_ref, me, ff), hid_v.at[me], local_sem.at[2])
    own_grad = pltpu.make_async_copy(gcols.at[me], cols(gr_ref, me, ff), local_sem.at[3])
    own_og.start()
    own_w.start()
    own_hid.start()

    barrier = pltpu.get_barrier_semaphore()

    @pl.loop(1, n)
    def _(k):
        pl.semaphore_signal(barrier, inc=1, device_id={"row": (me + k) % n}, device_id_type=MESH)

    pl.semaphore_wait(barrier, n - 1)

    def shard_copy(owner, target, send):
        return pltpu.make_async_remote_copy(
            og_all.at[owner], og_all.at[owner], send, ag_recv.at[owner],
            device_id={"row": target}, device_id_type=MESH,
        )

    def down(zp):
        return shard_copy(idx(zp, y, c), idx((z + A - 1) % A, y, c), z_send.at[zp])

    def up(zp):
        return shard_copy(idx(zp, y, c), idx((z + 1) % A, y, c), z_send.at[A + zp])

    def across(zp):
        return shard_copy(idx(zp, y, c), idx(z, (y + 1) % B, c), y_send.at[zp])

    def beside(zp, yp):
        return shard_copy(idx(zp, yp, c), idx(z, y, 1 - c), c_send.at[zp * B + yp])

    def hidden_copy(k):
        to = (me + k) % n
        return pltpu.make_async_remote_copy(
            cols(hid_ref, to, ff), hid_v.at[me], h_send.at[k], h_recv.at[me],
            device_id={"row": to}, device_id_type=MESH,
        )

    def grad_copy(owner):
        return pltpu.make_async_remote_copy(
            gcols.at[owner], cols(gr_ref, me, ff), g_send.at[owner], g_recv.at[me],
            device_id={"row": owner}, device_id_type=MESH,
        )

    def wait_shard(owner):
        pltpu.make_async_copy(og_all.at[owner], og_all.at[owner], ag_recv.at[owner]).wait()

    def forward(zp, first):
        if not first:
            wait_shard(idx(zp, y, c))

        @pl.when((zp >= z) & (z > 0))
        def _():
            down(zp).start()

        @pl.when((zp <= z) & (z < A - 1))
        def _():
            up(zp).start()

        if B > 1:
            across(zp).start()
        beside(zp, y).start()

    def forward_across(zp):
        if B > 1:
            other = (y + 1) % B
            wait_shard(idx(zp, other, c))
            beside(zp, other).start()

    def produce(zp):
        for yp in range(B):
            wait_shard(idx(zp, yp, 1 - c))
        block = pl.ds(pl.multiple_of(zp * 2 * B, 2 * B), 2 * B)
        gcols[block] = lax.dot_general(
            og_all[block].reshape(2 * B * rows, depth), w_v[...], (((1,), (1,)), ((), ())),
            preferred_element_type=jnp.float32,
        ).astype(gcols.dtype).reshape(2 * B, rows, ff)

        @pl.loop(0, 2 * B)
        def _(i):
            owner = zp * 2 * B + i

            @pl.when(owner == me)
            def _():
                own_grad.start()

            @pl.when(owner != me)
            def _():
                grad_copy(owner).start()

    own_og.wait()
    forward(z, True)

    @pl.loop(1, n)
    def _(k):
        hidden_copy(k).start()

    own_w.wait()

    @pl.loop(1, A + 1)
    def _(d):
        for sign in (1, -1):
            zp = z + sign * d

            @pl.when((d < A) & (zp >= 0) & (zp < A))
            def _():
                forward(zp, False)

        for sign in (1, -1):
            zp = z + sign * (d - 1)

            @pl.when(((d > 1) | (sign == 1)) & (zp >= 0) & (zp < A))
            def _():
                forward_across(zp)

        @pl.loop(0, 2)
        def _(j):
            zp = z + (1 - 2 * j) * (d - 1)

            @pl.when(((d > 1) | (j == 0)) & (zp >= 0) & (zp < A))
            def _():
                produce(zp)

    own_hid.wait()

    @pl.loop(0, n)
    def _(k):
        src = (me + k) % n

        @pl.when(k > 0)
        def _():
            pltpu.make_async_copy(hid_v.at[src], hid_v.at[src], h_recv.at[src]).wait()

        hid_t[:, pl.ds(pl.multiple_of(src * rows, 128), rows)] = hid_v[src].T

    def out_copy(t):
        at = pl.ds(pl.multiple_of(t * TILE, TILE), TILE)
        return pltpu.make_async_copy(wg_v.at[:, at], wg_ref.at[:, at], out_sem.at[t])

    @pl.loop(0, depth // TILE)
    def _(t):
        at = pl.ds(pl.multiple_of(t * TILE, TILE), TILE)
        wg_v[:, at] = lax.dot_general(
            hid_t[...], og_all[:, :, at].reshape(n * rows, TILE), (((1,), (0,)), ((), ())),
            preferred_element_type=jnp.float32,
        ).astype(wg_v.dtype)
        out_copy(t).start()

    @pl.loop(0, A)
    def _(zp):
        @pl.when((zp >= z) & (z > 0))
        def _():
            down(zp).wait_send()

        @pl.when((zp <= z) & (z < A - 1))
        def _():
            up(zp).wait_send()

        if B > 1:
            across(zp).wait_send()
        for yp in range(B):
            beside(zp, yp).wait_send()

    @pl.loop(0, depth // TILE)
    def _(t):
        out_copy(t).wait()

    @pl.loop(1, n)
    def _(k):
        hidden_copy(k).wait_send()
        grad_copy((me + k) % n).wait_send()

    own_grad.wait()

    @pl.loop(1, n)
    def _(k):
        src = (me + k) % n
        pltpu.make_async_copy(cols(gr_ref, src, ff), cols(gr_ref, src, ff), g_recv.at[src]).wait()


def local(n, gate_pre, up_pre, out_grad, down_weight):
    rows, width = gate_pre.shape
    ff, depth = down_weight.shape
    B = 2 if n == 16 else 1
    A = n // (2 * B)
    flat = ff % 128 == 0
    gate_wide = gate_pre.astype(jnp.float32)
    up_wide = up_pre.astype(jnp.float32)
    hidden = (jax.nn.silu(gate_wide) * up_wide).astype(jnp.bfloat16)
    if not flat:
        hidden = hidden.reshape(rows, n, ff).transpose(1, 0, 2)
    bf16 = jnp.bfloat16
    dma = pltpu.SemaphoreType.DMA
    weight_grad, grad_rows = pl.pallas_call(
        functools.partial(kernel, A, B),
        out_shape=(
            jax.ShapeDtypeStruct((ff, depth), bf16),
            jax.ShapeDtypeStruct((rows, width) if flat else (n, rows, ff), bf16),
        ),
        in_specs=[pl.BlockSpec(memory_space=pl.ANY)] * 3,
        out_specs=(pl.BlockSpec(memory_space=pl.ANY),) * 2,
        scratch_shapes=[
            pltpu.VMEM((n, rows, depth), bf16),
            pltpu.VMEM((ff, depth), bf16),
            pltpu.VMEM((n, rows, ff), bf16),
            pltpu.VMEM((ff, n * rows), bf16),
            pltpu.VMEM((n, rows, ff), bf16),
            pltpu.VMEM((ff, depth), bf16),
            dma((4,)),
            dma((n,)),
            dma((2 * A,)),
            dma((A,)),
            dma((n // 2,)),
            dma((n,)),
            dma((n,)),
            dma((n,)),
            dma((n,)),
            dma((depth // TILE,)),
        ],
        compiler_params=pltpu.CompilerParams(
            collective_id=0, has_side_effects=True, vmem_limit_bytes=60 * 2**20
        ),
        name="swiglu_backward",
    )(hidden, out_grad, down_weight)
    if not flat:
        grad_rows = grad_rows.transpose(1, 0, 2).reshape(rows, width)
    grad_wide = grad_rows.astype(jnp.float32)
    sigmoid = 1.0 / (1.0 + jnp.exp(-gate_wide))
    up_grad = (grad_wide * gate_wide * sigmoid).astype(bf16)
    gate_grad = (grad_wide * up_wide * sigmoid * (1.0 + gate_wide * (1.0 - sigmoid))).astype(bf16)
    return (weight_grad, gate_grad, up_grad)


def solution(mesh):
    return jax.shard_map(
        functools.partial(local, mesh.shape["row"]),
        mesh=mesh,
        in_specs=(
            P(("groups", "row"), None),
            P(("groups", "row"), None),
            P(("groups", "row"), None),
            P("row", None),
        ),
        out_specs=(
            P(("groups", "row"), None),
            P(("groups", "row"), None),
            P(("groups", "row"), None),
        ),
        check_vma=False,
    )
```

```python
import functools

import jax
import jax.numpy as jnp
from jax import lax
from jax.experimental import pallas as pl
from jax.experimental.pallas import tpu as pltpu
from jax.sharding import PartitionSpec as P

MESH = pl.DeviceIdType.MESH
TILE = 256
PARTS = 4
EARLY = 0
MORE = 2


def cols(ref, at, ff):
    if len(ref.shape) == 3:
        return ref.at[at]
    return ref.at[:, pl.ds(pl.multiple_of(at * ff, 128), ff)]


def kernel(
    A, B, hid_ref, og_ref, w_ref, wg_ref, gr_ref, og_all, w_v, hid_v, hid_t, gcols, wg_v,
    local_sem, ag_recv, z_send, y_send, c_send, h_send, h_recv, g_send, g_recv, out_sem,
):
    n = A * B * 2
    ff, depth = w_ref.shape
    rows = og_ref.shape[0]
    me = lax.axis_index("row")
    z, y, c = me // (2 * B), (me // 2) % B, me % 2

    def idx(zz, yy, cc):
        return (zz * B + yy) * 2 + cc

    own_og = pltpu.make_async_copy(og_ref, og_all.at[me], local_sem.at[0])
    own_w = pltpu.make_async_copy(w_ref, w_v, local_sem.at[1])
    own_hid = pltpu.make_async_copy(cols(hid_ref, me, ff), hid_v.at[me], local_sem.at[2])
    own_grad = pltpu.make_async_copy(gcols.at[me], cols(gr_ref, me, ff), local_sem.at[3])
    own_og.start()
    own_w.start()
    own_hid.start()

    barrier = pltpu.get_barrier_semaphore()

    @pl.loop(1, n)
    def _(k):
        pl.semaphore_signal(barrier, inc=1, device_id={"row": (me + k) % n}, device_id_type=MESH)

    pl.semaphore_wait(barrier, n - 1)

    part = rows // PARTS

    def piece(owner, q):
        return og_all.at[owner, pl.ds(pl.multiple_of(q * part, part), part)]

    def shard_copy(owner, q, target, send):
        return pltpu.make_async_remote_copy(
            piece(owner, q), piece(owner, q), send, ag_recv.at[owner * PARTS + q],
            device_id={"row": target}, device_id_type=MESH,
        )

    def down(zp, q):
        return shard_copy(idx(zp, y, c), q, idx((z + A - 1) % A, y, c), z_send.at[zp * PARTS + q])

    def up(zp, q):
        return shard_copy(
            idx(zp, y, c), q, idx((z + 1) % A, y, c), z_send.at[(A + zp) * PARTS + q]
        )

    def across(zp, q):
        return shard_copy(idx(zp, y, c), q, idx(z, (y + 1) % B, c), y_send.at[zp * PARTS + q])

    def beside(zp, yp, q):
        return shard_copy(
            idx(zp, yp, c), q, idx(z, y, 1 - c), c_send.at[(zp * B + yp) * PARTS + q]
        )

    def hidden_copy(k):
        to = (me + k * (7 if n % 7 else 1)) % n
        return pltpu.make_async_remote_copy(
            cols(hid_ref, to, ff), hid_v.at[me], h_send.at[k], h_recv.at[me],
            device_id={"row": to}, device_id_type=MESH,
        )

    def grad_copy(owner):
        return pltpu.make_async_remote_copy(
            gcols.at[owner], cols(gr_ref, me, ff), g_send.at[owner], g_recv.at[me],
            device_id={"row": owner}, device_id_type=MESH,
        )

    def wait_piece(owner, q):
        pltpu.make_async_copy(
            piece(owner, q), piece(owner, q), ag_recv.at[owner * PARTS + q]
        ).wait()

    def forward(zp, q, first):
        if not first:
            wait_piece(idx(zp, y, c), q)

        @pl.when((zp >= z) & (z > 0))
        def _():
            down(zp, q).start()

        @pl.when((zp <= z) & (z < A - 1))
        def _():
            up(zp, q).start()

        if B > 1:
            across(zp, q).start()
        beside(zp, y, q).start()

    def forward_across(zp, q):
        if B > 1:
            other = (y + 1) % B
            wait_piece(idx(zp, other, c), q)
            beside(zp, other, q).start()

    def produce(zp):
        for yp in range(B):
            for q in range(PARTS):
                wait_piece(idx(zp, yp, 1 - c), q)
        block = pl.ds(pl.multiple_of(zp * 2 * B, 2 * B), 2 * B)
        gcols[block] = lax.dot_general(
            og_all[block].reshape(2 * B * rows, depth), w_v[...], (((1,), (1,)), ((), ())),
            preferred_element_type=jnp.float32,
        ).astype(gcols.dtype).reshape(2 * B, rows, ff)

        @pl.loop(0, 2 * B)
        def _(i):
            owner = zp * 2 * B + i

            @pl.when(owner == me)
            def _():
                own_grad.start()

            @pl.when(owner != me)
            def _():
                grad_copy(owner).start()

    own_og.wait()

    @pl.loop(0, PARTS)
    def _(q):
        forward(z, q, True)

    early = min(EARLY, n - 1)

    @pl.loop(1, 1 + early)
    def _(k):
        hidden_copy(k).start()

    share = max(MORE, -(-(n - 1 - early) // (A * PARTS)))
    own_w.wait()

    @pl.loop(1, A + 1)
    def _(d):
        @pl.loop(0, PARTS)
        def _(q):
            for sign in (1, -1):
                zp = z + sign * d

                @pl.when((d < A) & (zp >= 0) & (zp < A))
                def _():
                    forward(zp, q, False)

            @pl.loop(0, share)
            def _(i):
                k = ((d - 1) * PARTS + q) * share + i + 1 + early

                @pl.when(k < n)
                def _():
                    hidden_copy(k).start()

            for sign in (1, -1):
                zp = z + sign * (d - 1)

                @pl.when(((d > 1) | (sign == 1)) & (zp >= 0) & (zp < A))
                def _():
                    forward_across(zp, q)

        @pl.loop(0, 2)
        def _(j):
            zp = z + (1 - 2 * j) * (d - 1)

            @pl.when(((d > 1) | (j == 0)) & (zp >= 0) & (zp < A))
            def _():
                produce(zp)

    own_hid.wait()

    @pl.loop(0, n)
    def _(k):
        src = (me + k) % n

        @pl.when(k > 0)
        def _():
            pltpu.make_async_copy(hid_v.at[src], hid_v.at[src], h_recv.at[src]).wait()

        hid_t[:, pl.ds(pl.multiple_of(src * rows, 128), rows)] = hid_v[src].T

    def out_copy(t):
        at = pl.ds(pl.multiple_of(t * TILE, TILE), TILE)
        return pltpu.make_async_copy(wg_v.at[:, at], wg_ref.at[:, at], out_sem.at[t])

    @pl.loop(0, depth // TILE)
    def _(t):
        at = pl.ds(pl.multiple_of(t * TILE, TILE), TILE)
        wg_v[:, at] = lax.dot_general(
            hid_t[...], og_all[:, :, at].reshape(n * rows, TILE), (((1,), (0,)), ((), ())),
            preferred_element_type=jnp.float32,
        ).astype(wg_v.dtype)
        out_copy(t).start()

    @pl.loop(0, A * PARTS)
    def _(e):
        zp, q = e // PARTS, e % PARTS

        @pl.when((zp >= z) & (z > 0))
        def _():
            down(zp, q).wait_send()

        @pl.when((zp <= z) & (z < A - 1))
        def _():
            up(zp, q).wait_send()

        if B > 1:
            across(zp, q).wait_send()
        for yp in range(B):
            beside(zp, yp, q).wait_send()

    @pl.loop(0, depth // TILE)
    def _(t):
        out_copy(t).wait()

    @pl.loop(1, n)
    def _(k):
        hidden_copy(k).wait_send()
        grad_copy((me + k) % n).wait_send()

    own_grad.wait()

    @pl.loop(1, n)
    def _(k):
        src = (me + k) % n
        pltpu.make_async_copy(cols(gr_ref, src, ff), cols(gr_ref, src, ff), g_recv.at[src]).wait()


def local(n, gate_pre, up_pre, out_grad, down_weight):
    rows, width = gate_pre.shape
    ff, depth = down_weight.shape
    B = 2 if n == 16 else 1
    A = n // (2 * B)
    flat = ff % 128 == 0
    gate_wide = gate_pre.astype(jnp.float32)
    up_wide = up_pre.astype(jnp.float32)
    hidden = (jax.nn.silu(gate_wide) * up_wide).astype(jnp.bfloat16)
    if not flat:
        hidden = hidden.reshape(rows, n, ff).transpose(1, 0, 2)
    bf16 = jnp.bfloat16
    dma = pltpu.SemaphoreType.DMA
    weight_grad, grad_rows = pl.pallas_call(
        functools.partial(kernel, A, B),
        out_shape=(
            jax.ShapeDtypeStruct((ff, depth), bf16),
            jax.ShapeDtypeStruct((rows, width) if flat else (n, rows, ff), bf16),
        ),
        in_specs=[pl.BlockSpec(memory_space=pl.ANY)] * 3,
        out_specs=(pl.BlockSpec(memory_space=pl.ANY),) * 2,
        scratch_shapes=[
            pltpu.VMEM((n, rows, depth), bf16),
            pltpu.VMEM((ff, depth), bf16),
            pltpu.VMEM((n, rows, ff), bf16),
            pltpu.VMEM((ff, n * rows), bf16),
            pltpu.VMEM((n, rows, ff), bf16),
            pltpu.VMEM((ff, depth), bf16),
            dma((4,)),
            dma((n * PARTS,)),
            dma((2 * A * PARTS,)),
            dma((A * PARTS,)),
            dma((n // 2 * PARTS,)),
            dma((n,)),
            dma((n,)),
            dma((n,)),
            dma((n,)),
            dma((depth // TILE,)),
        ],
        compiler_params=pltpu.CompilerParams(
            collective_id=0, has_side_effects=True, vmem_limit_bytes=60 * 2**20
        ),
        name="swiglu_backward",
    )(hidden, out_grad, down_weight)
    if not flat:
        grad_rows = grad_rows.transpose(1, 0, 2).reshape(rows, width)
    grad_wide = grad_rows.astype(jnp.float32)
    sigmoid = 1.0 / (1.0 + jnp.exp(-gate_wide))
    up_grad = (grad_wide * gate_wide * sigmoid).astype(bf16)
    gate_grad = (grad_wide * up_wide * sigmoid * (1.0 + gate_wide * (1.0 - sigmoid))).astype(bf16)
    return (weight_grad, gate_grad, up_grad)


def solution(mesh):
    return jax.shard_map(
        functools.partial(local, mesh.shape["row"]),
        mesh=mesh,
        in_specs=(
            P(("groups", "row"), None),
            P(("groups", "row"), None),
            P(("groups", "row"), None),
            P("row", None),
        ),
        out_specs=(
            P(("groups", "row"), None),
            P(("groups", "row"), None),
            P(("groups", "row"), None),
        ),
        check_vma=False,
    )
```
